1024 devices in a mesh: prow: 16 (over y_hi, x, core), pcol: 64 (over y_lo, z).
Axes of the slice: x: 4, y: 4 (y_hi: 2, y_lo: 2; y = y_hi * 2 + y_lo), z: 32, core: 2. Of those that a mesh axis runs over, the one named last changes fastest.
Arguments:
- trailing: bfloat16 [8192, 65536], P('prow', 'pcol'), may hold values from -6 to 6
- lower_raw: bfloat16 [8192, 512], P(('prow', 'pcol')), may hold values from -0.25 to 0.25
- upper_raw: bfloat16 [512, 65536], P('prow', 'pcol'), may hold values from -6 to 6
- lower_inv: bfloat16 [512, 512], replicated, as said below
- upper_inv: bfloat16 [512, 512], replicated, as said below
Outputs:
- updated: bfloat16 [8192, 65536], P('prow', 'pcol')
The draws below stay inside these ranges and needn't reach their ends.
Inputs may be any that keep to these rules, and one draw needn't show every extreme that they name: lower_inv is unit lower triangular. upper_inv is upper triangular with a positive diagonal.
All inputs are finite; a program needn't handle non-finite values.
Results may differ from the reference program's by a relative error of at most 0.0052.
Values may be sent and summed in bfloat16 or wider, within the bound.
No kernel may reach another device: no remote copies, remote signals or barrier semaphores. Data moves between devices by JAX's collectives and lax.ppermute only.
A program may use at most 32 MiB of HBM per device.

```python
import jax
import jax.numpy as jnp
from jax import lax

NB = 512
ROWS = 8192
COLS = 65536


def triangle_terms(key, spread):
    noise = jax.random.normal(key, (NB, NB), jnp.float32)
    return noise * (spread / NB ** 0.5)


def draw_lower_inv(key, part):
    key = jax.random.fold_in(key, 11)
    row_ids = jnp.arange(NB)[:, None]
    col_ids = jnp.arange(NB)[None, :]
    terms = triangle_terms(key, 0.5)
    whole = jnp.where(row_ids > col_ids, terms, 0.0) + jnp.where(row_ids == col_ids, 1.0, 0.0)
    return whole.astype(jnp.bfloat16)


def draw_upper_inv(key, part):
    key = jax.random.fold_in(key, 23)
    first, second = jax.random.split(key)
    row_ids = jnp.arange(NB)[:, None]
    col_ids = jnp.arange(NB)[None, :]
    terms = triangle_terms(first, 0.5)
    diag_vals = jax.random.uniform(second, (NB, 1), jnp.float32, 0.6, 1.6)
    whole = jnp.where(row_ids < col_ids, terms, 0.0) + jnp.where(row_ids == col_ids, diag_vals, 0.0)
    return whole.astype(jnp.bfloat16)


def shard_levels(key, extent, cuts, least, top_value):
    level = 1.0
    for position, shards_of in cuts:
        draws = jax.random.uniform(jax.random.fold_in(jax.random.fold_in(key, 6), position), (shards_of,), jnp.float32, least / len(cuts), top_value / len(cuts))
        level = level * jnp.repeat(jnp.exp(draws), extent[position] // shards_of).reshape((-1,) + (1,) * (len(extent) - 1 - position))
    return level


def gaussian(key, dims, scale, reach, cuts=(), kind=jnp.bfloat16):
    array = jax.random.normal(key, dims, jnp.float32) * scale
    if len(cuts) > 0:
        array = shard_levels(key, dims, cuts, -0.22, 0.18) * array
    return jnp.clip(array, min=-reach, max=reach).astype(kind)


def setup_inputs(seed: int = 0) -> dict:
    splits = jax.random.split(jax.random.key(seed), 6)
    return {
        "trailing": gaussian(splits[0], (ROWS, COLS), 1.0, 6.0, ((0, 16), (1, 64))),
        "lower_raw": gaussian(splits[1], (ROWS, NB), NB ** -0.5, 0.25, ((0, 1024),)),
        "upper_raw": gaussian(splits[2], (NB, COLS), 1.0, 6.0, ((0, 16), (1, 64))),
        "lower_inv": draw_lower_inv(jax.random.fold_in(splits[5], 71), 0),
        "upper_inv": draw_upper_inv(jax.random.fold_in(splits[5], 71), 0),
    }


def reference(trailing, lower_raw, upper_raw, lower_inv, upper_inv):
    lower_panel = jnp.dot(lower_raw, upper_inv, preferred_element_type=jnp.float32).astype(jnp.bfloat16)
    upper_panel = jnp.dot(lower_inv, upper_raw, preferred_element_type=jnp.float32).astype(jnp.bfloat16)
    tile_rows = trailing.reshape(ROWS // NB, NB, COLS)
    panel_rows = lower_panel.reshape(ROWS // NB, NB, NB)

    def one_tile(pair):
        block, panel = pair
        product = jnp.dot(panel, upper_panel, preferred_element_type=jnp.float32)
        return (block.astype(jnp.float32) - product).astype(jnp.bfloat16)

    result = lax.map(one_tile, (tile_rows, panel_rows))
    return result.reshape(ROWS, COLS)
```

```python
import jax
import jax.numpy as jnp
from jax import lax
from jax.sharding import Mesh, PartitionSpec as P

AXES = ("y_hi", "x", "core", "y_lo", "z_far", "z_near")
SIZES = (2, 4, 2, 2, 16, 2)
FAR, NEAR = SIZES[4], SIZES[5]


def share(block, axes, count):
    copies = jnp.broadcast_to(block[None], (count,) + block.shape)
    return lax.all_to_all(copies, axes, 0, 0)


def on_device(trailing, lower_raw, upper_raw, lower_inv, upper_inv):
    far = share(lower_raw, "z_far", FAR)
    core = lax.axis_index("core")
    upper = lax.all_gather(upper_raw, "y_hi", axis=0)
    upper = lax.all_gather(upper, "x", axis=0).reshape(256, 1024)
    far, upper = lax.optimization_barrier((far, upper))
    near = share(far.reshape(FAR * 8, 512), ("y_lo", "z_near"), 2 * NEAR)
    other = lax.ppermute(upper, "core", [(0, 1), (1, 0)])
    inverse = lower_inv.reshape(512, 2, 4, 2, 32)
    inverse = inverse.transpose(3, 0, 2, 1, 4).reshape(2, 512, 256)
    mine = lax.dynamic_index_in_dim(inverse, core, 0, keepdims=False)
    theirs = lax.dynamic_index_in_dim(inverse, 1 - core, 0, keepdims=False)
    upper_panel = (
        jnp.dot(mine, upper, preferred_element_type=jnp.float32)
        + jnp.dot(theirs, other, preferred_element_type=jnp.float32)
    ).astype(jnp.bfloat16)
    lower = jnp.swapaxes(near.reshape(2, NEAR, FAR, 8, 512), 1, 2).reshape(512, 512)
    solved = jnp.dot(lower, upper_inv, preferred_element_type=jnp.float32).astype(jnp.bfloat16)
    product = jnp.dot(solved, upper_panel, preferred_element_type=jnp.float32)
    return (trailing.astype(jnp.float32) - product).astype(jnp.bfloat16)


def solution(mesh):
    mesh = Mesh(mesh.devices.reshape(SIZES), AXES)
    rows, columns = AXES[:3], AXES[3:]
    in_specs = (P(rows, columns), P(AXES, None), P(rows, columns), P(), P())
    return jax.shard_map(
        on_device, mesh=mesh, in_specs=in_specs, out_specs=P(rows, columns), check_vma=False
    )
```

```python
import functools

import jax
import jax.numpy as jnp
from jax import lax
from jax.experimental import pallas as pl
from jax.experimental.pallas import tpu as pltpu
from jax.sharding import Mesh, PartitionSpec as P

AXES = ("y_hi", "x", "core", "y_lo", "z")
SIZES = (2, 4, 2, 2, 32)
NEAR = 2
FAR = 32 // NEAR
FIRST = 24
ORDER = [(FIRST + NEAR * i) % 32 // NEAR for i in range(FAR)]
GROUPS = [[NEAR * i + j for i in ORDER] for j in range(NEAR)]
SWAP = [(0, 1), (1, 0)]
ROWS = FAR * 8


def gather_far(block):
    copies = jnp.broadcast_to(block[None], (FAR,) + block.shape)
    return lax.all_to_all(copies, "z", 0, 0, axis_index_groups=GROUPS)


def gather_near(block):
    copies = jnp.broadcast_to(block[None], (2 * NEAR,) + block.shape)
    groups = [
        [32 * y + NEAR * i + j for y in range(2) for j in range(NEAR)] for i in range(FAR)
    ]
    return lax.all_to_all(copies, ("y_lo", "z"), 0, 0, axis_index_groups=groups)


def update(parts_ref, inverse_ref, upper_ref, trailing_ref, out_ref, solved, done, sems):
    for part in range(2 * NEAR):
        rows = jnp.dot(parts_ref[part], inverse_ref[...], preferred_element_type=jnp.float32)
        for i, place in enumerate(ORDER):
            at = 8 * (32 * (part // NEAR) + NEAR * place + part % NEAR)
            solved[pl.ds(at, 8), :] = rows[i * 8 : i * 8 + 8]
    copies = []
    for step in range(4):
        rows = pl.ds(step * 128, 128)
        product = jnp.dot(
            solved[rows, :].astype(jnp.bfloat16), upper_ref[...], preferred_element_type=jnp.float32
        )
        done[rows, :] = (trailing_ref[rows, :].astype(jnp.float32) - product).astype(jnp.bfloat16)
        copies.append(pltpu.make_async_copy(done.at[rows, :], out_ref.at[rows, :], sems.at[step]))
        copies[-1].start()
    for copy in copies:
        copy.wait()


def on_device(trailing, lower_raw, upper_raw, lower_inv, upper_inv):
    core = lax.axis_index("core")
    y_hi = lax.axis_index("y_hi")
    far = gather_far(lower_raw)
    upper = lax.all_gather(upper_raw, "y_hi", axis=0)
    upper = lax.all_gather(upper, "x", axis=0).reshape(256, 1024)
    far, upper = lax.optimization_barrier((far, upper))
    parts = gather_near(far.reshape(ROWS, 512))
    other = lax.ppermute(upper, "core", SWAP)
    inverse = lower_inv.reshape(512, 2, 4, 2, 32)
    inverse = inverse.transpose(3, 0, 2, 1, 4).reshape(2, 512, 256)
    mine = lax.dynamic_index_in_dim(inverse, core, 0, keepdims=False)
    theirs = lax.dynamic_index_in_dim(inverse, 1 - core, 0, keepdims=False)
    upper_panel = (
        jnp.dot(mine, upper, preferred_element_type=jnp.float32)
        + jnp.dot(theirs, other, preferred_element_type=jnp.float32)
    ).astype(jnp.bfloat16)
    whole = pl.BlockSpec(memory_space=pltpu.VMEM)
    return pl.pallas_call(
        update,
        out_shape=jax.ShapeDtypeStruct((512, 1024), jnp.bfloat16),
        in_specs=[whole, whole, whole, whole],
        out_specs=pl.BlockSpec(memory_space=pl.ANY),
        scratch_shapes=[
            pltpu.VMEM((512, 512), jnp.float32),
            pltpu.VMEM((512, 1024), jnp.bfloat16),
            pltpu.SemaphoreType.DMA((4,)),
        ],
        compiler_params=pltpu.CompilerParams(vmem_limit_bytes=24 * 2**20),
        cost_estimate=pl.CostEstimate(
            flops=2 * 512 * 512 * 1536, bytes_accessed=4 * 2**20, transcendentals=0
        ),
        name="update",
    )(parts, upper_inv, upper_panel, trailing)


def solution(mesh):
    mesh = Mesh(mesh.devices.reshape(SIZES), AXES)
    rows, columns = AXES[:3], AXES[3:]
    in_specs = (P(rows, columns), P(AXES, None), P(rows, columns), P(), P())
    return jax.shard_map(
        on_device, mesh=mesh, in_specs=in_specs, out_specs=P(rows, columns), check_vma=False
    )
```

```python
import functools

import jax
import jax.numpy as jnp
from jax import lax
from jax.experimental import pallas as pl
from jax.experimental.pallas import tpu as pltpu
from jax.sharding import Mesh, PartitionSpec as P

AXES = ("y_hi", "x", "core", "y_lo", "z")
SIZES = (2, 4, 2, 2, 32)
NEAR = 2
FAR = 32 // NEAR
FIRST = 22
ORDER = [(FIRST + NEAR * i) % 32 // NEAR for i in range(FAR)]
GROUPS = [[NEAR * i + j for i in ORDER] for j in range(NEAR)]
SWAP = [(0, 1), (1, 0)]
ROWS = FAR * 8


def gather_far(block):
    copies = jnp.broadcast_to(block[None], (FAR,) + block.shape)
    return lax.all_to_all(copies, "z", 0, 0, axis_index_groups=GROUPS)


def gather_near(block):
    copies = jnp.broadcast_to(block[None], (2 * NEAR,) + block.shape)
    groups = [
        [32 * y + NEAR * i + j for y in range(2) for j in range(NEAR)] for i in range(FAR)
    ]
    return lax.all_to_all(copies, ("y_lo", "z"), 0, 0, axis_index_groups=groups)


def update(parts_ref, inverse_ref, upper_ref, trailing_ref, out_ref, solved, done, sems):
    for part in range(2 * NEAR):
        rows = jnp.dot(parts_ref[part], inverse_ref[...], preferred_element_type=jnp.float32)
        for i, place in enumerate(ORDER):
            at = 8 * (32 * (part // NEAR) + NEAR * place + part % NEAR)
            solved[pl.ds(at, 8), :] = rows[i * 8 : i * 8 + 8]
    copies = []
    for step in range(4):
        rows = pl.ds(step * 128, 128)
        product = jnp.dot(
            solved[rows, :].astype(jnp.bfloat16), upper_ref[...], preferred_element_type=jnp.float32
        )
        done[rows, :] = (trailing_ref[rows, :].astype(jnp.float32) - product).astype(jnp.bfloat16)
        copies.append(pltpu.make_async_copy(done.at[rows, :], out_ref.at[rows, :], sems.at[step]))
        copies[-1].start()
    for copy in copies:
        copy.wait()


def on_device(trailing, lower_raw, upper_raw, lower_inv, upper_inv):
    core = lax.axis_index("core")
    y_hi = lax.axis_index("y_hi")
    far = gather_far(lower_raw)
    upper = lax.all_gather(upper_raw, "y_hi", axis=0)
    upper = lax.all_gather(upper, "x", axis=0).reshape(256, 1024)
    far, upper = lax.optimization_barrier((far, upper))
    parts = gather_near(far.reshape(ROWS, 512))
    other = lax.ppermute(upper, "core", SWAP)
    inverse = lower_inv.reshape(512, 2, 4, 2, 32)
    inverse = inverse.transpose(3, 0, 2, 1, 4).reshape(2, 512, 256)
    mine = lax.dynamic_index_in_dim(inverse, core, 0, keepdims=False)
    theirs = lax.dynamic_index_in_dim(inverse, 1 - core, 0, keepdims=False)
    upper_panel = (
        jnp.dot(mine, upper, preferred_element_type=jnp.float32)
        + jnp.dot(theirs, other, preferred_element_type=jnp.float32)
    ).astype(jnp.bfloat16)
    whole = pl.BlockSpec(memory_space=pltpu.VMEM)
    return pl.pallas_call(
        update,
        out_shape=jax.ShapeDtypeStruct((512, 1024), jnp.bfloat16),
        in_specs=[whole, whole, whole, whole],
        out_specs=pl.BlockSpec(memory_space=pl.ANY),
        scratch_shapes=[
            pltpu.VMEM((512, 512), jnp.float32),
            pltpu.VMEM((512, 1024), jnp.bfloat16),
            pltpu.SemaphoreType.DMA((4,)),
        ],
        compiler_params=pltpu.CompilerParams(vmem_limit_bytes=24 * 2**20),
        cost_estimate=pl.CostEstimate(
            flops=2 * 512 * 512 * 1536, bytes_accessed=4 * 2**20, transcendentals=0
        ),
        name="update",
    )(parts, upper_inv, upper_panel, trailing)


def solution(mesh):
    mesh = Mesh(mesh.devices.reshape(SIZES), AXES)
    rows, columns = AXES[:3], AXES[3:]
    in_specs = (P(rows, columns), P(AXES, None), P(rows, columns), P(), P())
    return jax.shard_map(
        on_device, mesh=mesh, in_specs=in_specs, out_specs=P(rows, columns), check_vma=False
    )
```

```python
import jax
import jax.numpy as jnp
from jax import lax
from jax.experimental import pallas as pl
from jax.experimental.pallas import tpu as pltpu
from jax.sharding import Mesh, PartitionSpec as P

AXES = ("y_hi", "x", "core", "y_lo", "z")
SIZES = (2, 4, 2, 2, 32)
NEAR = 2
FAR = 32 // NEAR
FIRST = 22
ORDER = [(FIRST + NEAR * i) % 32 // NEAR for i in range(FAR)]
GROUPS = [[NEAR * i + j for i in ORDER] for j in range(NEAR)]
SWAP = [(0, 1), (1, 0)]
ROWS = FAR * 8


def gather_far(block):
    copies = jnp.broadcast_to(block[None], (FAR,) + block.shape)
    return lax.all_to_all(copies, "z", 0, 0, axis_index_groups=GROUPS)


def gather_near(block):
    copies = jnp.broadcast_to(block[None], (2 * NEAR,) + block.shape)
    groups = [
        [32 * y + NEAR * i + j for y in range(2) for j in range(NEAR)] for i in range(FAR)
    ]
    return lax.all_to_all(copies, ("y_lo", "z"), 0, 0, axis_index_groups=groups)


def update(parts_ref, inverse_ref, upper_ref, trailing_ref, out_ref, solved, done, sems):
    for part in range(2 * NEAR):
        rows = jnp.dot(parts_ref[part], inverse_ref[...], preferred_element_type=jnp.float32)
        for i, place in enumerate(ORDER):
            at = 8 * (32 * (part // NEAR) + NEAR * place + part % NEAR)
            solved[pl.ds(at, 8), :] = rows[i * 8 : i * 8 + 8]
    copies = []
    for step in range(4):
        rows = pl.ds(step * 128, 128)
        product = jnp.dot(
            solved[rows, :].astype(jnp.bfloat16), upper_ref[...], preferred_element_type=jnp.float32
        )
        done[rows, :] = (trailing_ref[rows, :].astype(jnp.float32) - product).astype(jnp.bfloat16)
        copies.append(pltpu.make_async_copy(done.at[rows, :], out_ref.at[rows, :], sems.at[step]))
        copies[-1].start()
    for copy in copies:
        copy.wait()


def on_device(trailing, lower_raw, upper_raw, lower_inv, upper_inv):
    core = lax.axis_index("core")
    far = gather_far(lower_raw)
    upper = lax.all_gather(upper_raw, "y_hi", axis=0, tiled=True)
    upper = lax.all_gather(upper, "x", axis=0, tiled=True)
    far, upper = lax.optimization_barrier((far, upper))
    parts = gather_near(far.reshape(ROWS, 512))
    other = lax.ppermute(upper, "core", SWAP)
    inverse = lower_inv.reshape(512, 2, 4, 2, 32)
    inverse = inverse.transpose(3, 0, 2, 1, 4).reshape(2, 512, 256)
    mine = lax.dynamic_index_in_dim(inverse, core, 0, keepdims=False)
    theirs = lax.dynamic_index_in_dim(inverse, 1 - core, 0, keepdims=False)
    upper_panel = (
        jnp.dot(mine, upper, preferred_element_type=jnp.float32)
        + jnp.dot(theirs, other, preferred_element_type=jnp.float32)
    ).astype(jnp.bfloat16)
    whole = pl.BlockSpec(memory_space=pltpu.VMEM)
    return pl.pallas_call(
        update,
        out_shape=jax.ShapeDtypeStruct((512, 1024), jnp.bfloat16),
        in_specs=[whole, whole, whole, whole],
        out_specs=pl.BlockSpec(memory_space=pl.ANY),
        scratch_shapes=[
            pltpu.VMEM((512, 512), jnp.float32),
            pltpu.VMEM((512, 1024), jnp.bfloat16),
            pltpu.SemaphoreType.DMA((4,)),
        ],
        compiler_params=pltpu.CompilerParams(vmem_limit_bytes=24 * 2**20),
        cost_estimate=pl.CostEstimate(
            flops=2 * 512 * 512 * 1536, bytes_accessed=4 * 2**20, transcendentals=0
        ),
        name="update",
    )(parts, upper_inv, upper_panel, trailing)


def solution(mesh):
    mesh = Mesh(mesh.devices.reshape(SIZES), AXES)
    rows, columns = AXES[:3], AXES[3:]
    in_specs = (P(rows, columns), P(AXES, None), P(rows, columns), P(), P())
    return jax.shard_map(
        on_device, mesh=mesh, in_specs=in_specs, out_specs=P(rows, columns), check_vma=False
    )
```
